32 devices in a mesh: scan: 8 (over z, x), tile: 4 (over y, core).
Axes of the slice: x: 2, y: 2, z: 4, core: 2. Of those that a mesh axis runs over, the one named last changes fastest.
Arguments:
- probe_modes: float32 [3072, 256], P(('scan', 'tile')), may hold values from -2.1 to 2.1
- object_tiles: float32 [4, 2, 2, 320, 320], P('tile'), may hold values from -4 to 4
- scan_offsets: int32 [64, 2], P(('scan', 'tile')), may hold values from 0 to 64, as said below
- patch_tiles: int32 [64], P(('scan', 'tile')), may hold values from 0 to 3, as said below
- amplitudes: bfloat16 [64, 256, 256], P(('scan', 'tile')), may hold values from 0.5 to 20
Outputs:
- probe_gradient: float32 [3072, 256], P(('scan', 'tile'))
- object_gradient: float32 [4, 2, 2, 320, 320], P('tile', None, None, 'scan')
The draws below stay inside these ranges and needn't reach their ends.
Inputs may be any that keep to these rules, and one draw needn't show every extreme that they name: `patch_tiles`: each entry names the tile that wholly holds the patch of its position. `scan_offsets`: every patch lies wholly inside its tile.
All inputs are finite; a program needn't handle non-finite values.
Results may differ from the reference program's by a relative error of at most 0.02.
Values sent between devices are 32-bit elements; how exact they have to be, the bound alone decides.
A program may use at most 128 MiB of HBM per device.

```python
import math
import jax
import jax.numpy as jnp
from jax import lax

PROBE = 256
MODES = 6
SLICES = 2
POS_DEV = 2
TILE_SIDE = 320
TILES = 4
POSITIONS = 64


def heavy_device(key):
    device_total = POSITIONS // POS_DEV
    return jax.random.randint(jax.random.fold_in(key, 7), (), 0, device_total)


def position_device():
    return jnp.arange(POSITIONS, dtype=jnp.int32) // POS_DEV


def draw_patch_tiles(key, part):
    group_width = TILES * POS_DEV
    groups = POSITIONS // group_width
    key_list = jax.random.split(jax.random.fold_in(key, 11), 4)
    favourite = jax.random.randint(key_list[0], (groups, 1), 0, TILES)
    full_group = jax.random.randint(key_list[1], (), 0, groups)
    spread = jax.random.randint(key_list[2], (groups, group_width), 0, TILES)
    coin_flip = jax.random.randint(key_list[3], (groups, group_width), 0, 2)
    chosen = jnp.where(coin_flip == 1, favourite, spread)
    group_index = jnp.arange(groups, dtype=jnp.int32)[:, None]
    chosen = jnp.where(group_index == full_group, favourite, chosen).reshape(POSITIONS)
    heavy = heavy_device(key)
    chosen = jnp.where(position_device() == heavy, heavy % TILES, chosen)
    return chosen.astype(jnp.int32)


def draw_scan_offsets(key, part):
    key_list = jax.random.split(jax.random.fold_in(key, 13), 2)
    offsets = jax.random.randint(key_list[0], (POSITIONS, 2), 0, TILE_SIDE - PROBE + 1)
    heavy = heavy_device(key)
    scan_total = POSITIONS // (POS_DEV * TILES)
    row_count = TILE_SIDE // scan_total
    target = (heavy // TILES + scan_total // 2) % scan_total
    lowest = jnp.maximum(0, (target + 1) * row_count - PROBE)
    highest = jnp.minimum(target * row_count, TILE_SIDE - PROBE)
    planted = jax.random.randint(key_list[1], (POSITIONS,), lowest, highest + 1)
    rows = jnp.where(position_device() == heavy, planted, offsets[:, 0])
    return jnp.stack([rows, offsets[:, 1]], axis=1).astype(jnp.int32)


def draw_amplitudes(key, part):
    key_list = jax.random.split(jax.random.fold_in(key, 17), 2)
    drawn = jax.random.uniform(key_list[0], (POSITIONS, PROBE, PROBE), jnp.float32, 0.5, 2.5)
    strong = jax.random.uniform(key_list[1], (POSITIONS, PROBE, PROBE), jnp.float32, 12.0, 20.0)
    heavy = heavy_device(key)
    chosen = jnp.where((position_device() == heavy)[:, None, None], strong, drawn)
    return chosen.astype(jnp.bfloat16)


def block_scale(own_key, dims, cuts, low, largest):
    loudness = 1.0
    for position, shards_of in cuts:
        draws = jax.random.uniform(jax.random.fold_in(jax.random.fold_in(own_key, 6), position), (shards_of,), jnp.float32, low / len(cuts), largest / len(cuts))
        loudness = loudness * jnp.repeat(jnp.exp(draws), dims[position] // shards_of).reshape((-1,) + (1,) * (len(dims) - 1 - position))
    return loudness


def bell_draw(rng, shape, width, most, shards=(), held_as=jnp.bfloat16):
    entries = width * jax.random.normal(rng, shape, jnp.float32)
    if shards:
        entries = entries * block_scale(rng, shape, shards, -0.22, 0.18)
    return jnp.clip(entries, -most, most).astype(held_as)


def setup_inputs(seed: int = 0) -> dict:
    arg_keys = jax.random.split(jax.random.key(seed), 6)
    probe_modes = bell_draw(arg_keys[0], (2 * MODES * PROBE, PROBE), 0.35, 2.1, ((0, 32),), jnp.float32)
    object_tiles = bell_draw(arg_keys[1], (TILES, SLICES, 2, TILE_SIDE, TILE_SIDE), 0.7, 4.0, ((0, 4),), jnp.float32)
    scan_offsets = draw_scan_offsets(jax.random.fold_in(arg_keys[5], 71), 0)
    patch_tiles = draw_patch_tiles(jax.random.fold_in(arg_keys[5], 71), 0)
    amplitudes = draw_amplitudes(jax.random.fold_in(arg_keys[5], 71), 0)
    return {"probe_modes": probe_modes, "object_tiles": object_tiles, "scan_offsets": scan_offsets, "patch_tiles": patch_tiles, "amplitudes": amplitudes}


def complex_tables(pixels):
    pixel_index = jnp.arange(pixels, dtype=jnp.int32)
    offset = pixel_index[:, None] - pixel_index[None, :]
    chirp_phase = (offset * offset % (2 * pixels)).astype(jnp.float32) * (math.pi / pixels)
    product = (pixel_index[:, None] * pixel_index[None, :] % pixels).astype(jnp.float32) * (2.0 * math.pi / pixels)
    norm_scale = 1.0 / math.sqrt(pixels)
    fresnel = (jnp.stack([jnp.cos(chirp_phase), jnp.sin(chirp_phase)]) * norm_scale).astype(jnp.bfloat16)
    spectral = (jnp.stack([jnp.cos(product), -jnp.sin(product)]) * norm_scale).astype(jnp.bfloat16)
    return (fresnel, spectral)

def multiply_object(exit_wave, object_patch):
    real_part = exit_wave[0] * object_patch[0] - exit_wave[1] * object_patch[1]
    imag_part = exit_wave[0] * object_patch[1] + exit_wave[1] * object_patch[0]
    return jnp.stack([real_part, imag_part])

def left_side(matrix_part, component):
    return jnp.einsum('ij,mjk->mik', matrix_part.astype(jnp.float32), component.astype(jnp.float32), precision=lax.Precision.HIGHEST)

def right_side(component, matrix_part):
    return jnp.einsum('mik,jk->mij', component.astype(jnp.float32), matrix_part.astype(jnp.float32), precision=lax.Precision.HIGHEST)

def left_product(matrix, exit_wave):
    real_part = left_side(matrix[0], exit_wave[0]) - left_side(matrix[1], exit_wave[1])
    imag_part = left_side(matrix[0], exit_wave[1]) + left_side(matrix[1], exit_wave[0])
    return jnp.stack([real_part, imag_part])

def right_product(exit_wave, matrix):
    real_part = right_side(exit_wave[0], matrix[0]) - right_side(exit_wave[1], matrix[1])
    imag_part = right_side(exit_wave[0], matrix[1]) + right_side(exit_wave[1], matrix[0])
    return jnp.stack([real_part, imag_part])

def position_loss(probe_values, patch_values, amplitude, fresnel, spectral):
    exit_wave = probe_values
    layers = patch_values.shape[0]
    for slice_index in range(layers):
        exit_wave = multiply_object(exit_wave, patch_values[slice_index])
        matrix = fresnel if slice_index < layers - 1 else spectral
        rounded = exit_wave.astype(jnp.bfloat16)
        halfway = left_product(matrix, rounded).astype(jnp.bfloat16)
        exit_wave = right_product(halfway, matrix)
    intensity = lax.optimization_barrier(jnp.sum(exit_wave * exit_wave, axis=(0, 1)))
    residue = jnp.sqrt(intensity + 1.0) - amplitude.astype(jnp.float32)
    return jnp.sum(residue * residue)

def reference(probe_modes, object_tiles, scan_offsets, patch_tiles, amplitudes):
    pixels = probe_modes.shape[1]
    layers = object_tiles.shape[1]
    probe_field = probe_modes.astype(jnp.float32).reshape(2, -1, pixels, pixels)
    fresnel, spectral = complex_tables(pixels)

    def one_position(running, inputs):
        probe_total, object_total = running
        offsets, tile_number, amplitude = inputs
        corner = (tile_number.astype(jnp.int32), jnp.int32(0), jnp.int32(0), offsets[0].astype(jnp.int32), offsets[1].astype(jnp.int32))
        extent = (1, layers, 2, pixels, pixels)
        object_patch = lax.dynamic_slice(object_tiles, corner, extent)[0]

        def local_loss(probe_values, patch_values):
            return position_loss(probe_values, patch_values, amplitude, fresnel, spectral)
        misfit, pullback = jax.vjp(local_loss, probe_field, object_patch)
        probe_part, patch_part = pullback(jnp.ones_like(misfit))
        current = lax.dynamic_slice(object_total, corner, extent)
        object_total = lax.dynamic_update_slice(object_total, current + patch_part[None], corner)
        return ((probe_total + probe_part, object_total), None)
    initial = (jnp.zeros_like(probe_field), jnp.zeros(object_tiles.shape, jnp.float32))
    (probe_total, object_total), _ = lax.scan(one_position, initial, (scan_offsets, patch_tiles, amplitudes))
    return (probe_total.reshape(probe_modes.shape), object_total)
```

```python
import functools
import math

import jax
import jax.numpy as jnp
import ml_dtypes
import numpy as np
from jax import lax
from jax.experimental import pallas as pl
from jax.experimental.pallas import tpu as pltpu
from jax.sharding import PartitionSpec as P

MESH = pl.DeviceIdType.MESH
VMEM_BYTES = 56 * 1024 * 1024


def block_tables(pixels):
    index = np.arange(pixels, dtype=np.int64)
    offset = index[:, None] - index[None, :]
    chirp = (offset * offset % (2 * pixels)) * (math.pi / pixels)
    product = (index[:, None] * index[None, :] % pixels) * (2.0 * math.pi / pixels)
    scale = 1.0 / math.sqrt(pixels)
    tables = []
    for real, imag in ((np.cos(chirp), np.sin(chirp)), (np.cos(product), -np.sin(product))):
        real, imag = real * scale, imag * scale
        whole = np.block([[real, -imag], [imag, real]]).astype(np.float32)
        whole = whole.astype(ml_dtypes.bfloat16)
        tables += [whole, np.ascontiguousarray(whole.T)]
    return np.stack(tables)


def dot(left, right):
    return jnp.dot(left, right, preferred_element_type=jnp.float32)


def misfit_kernel(
    layers, group, tile_ref, corner_ref, probe_ref, object_ref, amplitude_ref, table_ref,
    probe_grad_ref, object_grad_ref, patch_ref, piece_ref, wave_ref, bright_ref,
):
    modes, pixels = probe_ref.shape[1], probe_ref.shape[2]
    positions = amplitude_ref.shape[0]
    planes, side = object_grad_ref.shape[0], object_grad_ref.shape[3]
    wide = -(-side // 128) * 128
    tall = min(pixels + 8, side)

    def clear(plane, carry):
        for tile in range(object_grad_ref.shape[1]):
            object_grad_ref[plane, tile] = jnp.zeros((side, side), jnp.float32)
        return carry

    lax.fori_loop(0, planes, clear, 0)

    def rows_of(value):
        return jnp.concatenate([value[:pixels], value[pixels:]], axis=1)

    def columns_of(value):
        return jnp.concatenate([value[:, :pixels], value[:, pixels:]], axis=0)

    def one_position(position, carry):
        tile = tile_ref[position]
        row, column = corner_ref[position, 0], corner_ref[position, 1]
        base = pl.multiple_of(jnp.minimum(row // 8 * 8, side - tall), 8)
        shift = row - base

        def cut(plane, carry):
            rows = object_ref[tile, plane, pl.ds(base, tall), :]
            padded = jnp.concatenate([rows, jnp.zeros((tall, wide - side), jnp.float32)], axis=1)
            moved = pltpu.roll(padded, lax.rem(wide - column, wide), 1)[:, :pixels]
            patch_ref[plane] = pltpu.roll(moved, lax.rem(tall - shift, tall), 0)[:pixels]
            piece_ref[plane] = jnp.zeros((pixels, pixels), jnp.float32)
            return carry

        lax.fori_loop(0, planes, cut, 0)
        bright_ref[...] = jnp.ones((pixels, pixels), jnp.float32)

        def incoming(layer, mode):
            if layer == 0:
                return probe_ref[0, mode], probe_ref[1, mode]
            return wave_ref[layer - 1, 0, mode], wave_ref[layer - 1, 1, mode]

        def table_at(layer):
            return 0 if layer < layers - 1 else 2

        def forward(step, carry):
            chosen = [step * group + member for member in range(group)]
            for layer in range(layers):
                at = table_at(layer)
                object_real, object_imag = patch_ref[2 * layer], patch_ref[2 * layer + 1]
                halves = []
                for mode in chosen:
                    real, imag = incoming(layer, mode)
                    rounded = jnp.concatenate(
                        [
                            real * object_real - imag * object_imag,
                            real * object_imag + imag * object_real,
                        ],
                        axis=0,
                    ).astype(jnp.bfloat16)
                    halves.append(dot(table_ref[at], rounded).astype(jnp.bfloat16))
                for mode, half in zip(chosen, halves):
                    wave = dot(rows_of(half), table_ref[at + 1])
                    real, imag = wave[:, :pixels], wave[:, pixels:]
                    wave_ref[layer, 0, mode] = real
                    wave_ref[layer, 1, mode] = imag
                    if layer == layers - 1:
                        bright_ref[...] += real * real + imag * imag
            return carry

        lax.fori_loop(0, modes // group, forward, 0)
        root = jnp.sqrt(bright_ref[...])
        measured = amplitude_ref[position].astype(jnp.float32)
        bright_ref[...] = 2.0 * (root - measured) / root

        def backward(step, carry):
            chosen = [step * group + member for member in range(group)]
            factor = bright_ref[...]
            cotangents = []
            for mode in chosen:
                real = wave_ref[layers - 1, 0, mode] * factor
                imag = wave_ref[layers - 1, 1, mode] * factor
                cotangents.append(jnp.concatenate([real, imag], axis=1).astype(jnp.bfloat16))
            for layer in reversed(range(layers)):
                at = table_at(layer)
                object_real, object_imag = patch_ref[2 * layer], patch_ref[2 * layer + 1]
                halves = [dot(value, table_ref[at]).astype(jnp.bfloat16) for value in cotangents]
                cotangents = []
                for mode, half in zip(chosen, halves):
                    change = dot(table_ref[at + 1], columns_of(half))
                    change = change.astype(jnp.bfloat16).astype(jnp.float32)
                    turn_real, turn_imag = change[:pixels], change[pixels:]
                    real, imag = incoming(layer, mode)
                    piece_ref[2 * layer] += turn_real * real + turn_imag * imag
                    piece_ref[2 * layer + 1] += turn_imag * real - turn_real * imag
                    back_real = turn_real * object_real + turn_imag * object_imag
                    back_imag = turn_imag * object_real - turn_real * object_imag
                    if layer > 0:
                        cotangents.append(
                            jnp.concatenate([back_real, back_imag], axis=1).astype(jnp.bfloat16)
                        )
                    else:
                        kept = position > 0
                        probe_grad_ref[0, mode] = back_real + jnp.where(
                            kept, probe_grad_ref[0, mode], 0.0
                        )
                        probe_grad_ref[1, mode] = back_imag + jnp.where(
                            kept, probe_grad_ref[1, mode], 0.0
                        )
            return carry

        lax.fori_loop(0, modes // group, backward, 0)

        def paste(plane, carry):
            padded = jnp.concatenate(
                [piece_ref[plane], jnp.zeros((tall - pixels, pixels), jnp.float32)], axis=0
            )
            moved = jnp.concatenate(
                [pltpu.roll(padded, shift, 0), jnp.zeros((tall, wide - pixels), jnp.float32)],
                axis=1,
            )
            moved = pltpu.roll(moved, column, 1)[:, :side]
            window = (plane, tile, pl.ds(base, tall), slice(None))
            object_grad_ref[window] = object_grad_ref[window] + moved
            return carry

        lax.fori_loop(0, planes, paste, 0)
        return carry

    lax.fori_loop(0, positions, one_position, 0)


def misfit_gradients(probe_field, whole_object, scan_offsets, patch_tiles, amplitudes):
    _, modes, pixels, _ = probe_field.shape
    tiles, planes, side, _ = whole_object.shape
    layers = planes // 2
    group = next(size for size in (3, 2, 1) if modes % size == 0)
    in_vmem = pl.BlockSpec(memory_space=pltpu.VMEM)
    in_smem = pl.BlockSpec(memory_space=pltpu.SMEM)
    return pl.pallas_call(
        functools.partial(misfit_kernel, layers, group),
        out_shape=(
            jax.ShapeDtypeStruct((2, modes, pixels, pixels), jnp.float32),
            jax.ShapeDtypeStruct((planes, tiles, side, side), jnp.float32),
        ),
        in_specs=[in_smem, in_smem, in_vmem, in_vmem, in_vmem, in_vmem],
        out_specs=(in_vmem, in_vmem),
        scratch_shapes=[
            pltpu.VMEM((planes, pixels, pixels), jnp.float32),
            pltpu.VMEM((planes, pixels, pixels), jnp.float32),
            pltpu.VMEM((layers, 2, modes, pixels, pixels), jnp.float32),
            pltpu.VMEM((pixels, pixels), jnp.float32),
        ],
        compiler_params=pltpu.CompilerParams(vmem_limit_bytes=VMEM_BYTES),
        name="misfit",
    )(
        patch_tiles, scan_offsets, probe_field, whole_object, amplitudes,
        jnp.asarray(block_tables(pixels)),
    )


class Cube:
    def __init__(self, scan_bits, tile_bits):
        scan, tile = lax.axis_index("scan"), lax.axis_index("tile")
        self.scan_names = ["s%d" % bit for bit in reversed(range(scan_bits))]
        self.tile_names = ["t%d" % bit for bit in reversed(range(tile_bits))]
        self.own, self.partner = {}, {}
        for axis, letter, index, bits in (("scan", "s", scan, scan_bits), ("tile", "t", tile, tile_bits)):
            for bit in range(bits):
                value = (index // (1 << bit)) % 2
                self.own[letter + str(bit)] = value
                self.partner[letter + str(bit)] = {axis: index + (1 - 2 * value) * (1 << bit)}

    def greet(self):
        barrier = pltpu.get_barrier_semaphore()
        for target in self.partner.values():
            pl.semaphore_signal(barrier, inc=1, device_id=target, device_id_type=MESH)
        pl.semaphore_wait(barrier, len(self.partner))


class Wires:
    def __init__(self, cube, send_sem, recv_sem):
        self.cube, self.send_sem, self.recv_sem, self.used = cube, send_sem, recv_sem, 0
        self.sent = []

    def start(self, source, target, name):
        copy = pltpu.make_async_remote_copy(
            src_ref=source,
            dst_ref=target,
            send_sem=self.send_sem.at[self.used],
            recv_sem=self.recv_sem.at[self.used],
            device_id=self.cube.partner[name],
            device_id_type=MESH,
        )
        self.used += 1
        copy.start()
        self.sent.append(copy)
        return copy

    def finish(self):
        for copy in self.sent:
            copy.wait_send()


def gather_kernel(
    scan_bits, tile_bits, probe_ref, object_ref, all_probe_ref, all_object_ref,
    send_sem, recv_sem, own_sem,
):
    cube = Cube(scan_bits, tile_bits)
    wires = Wires(cube, send_sem, recv_sem)
    own = cube.own
    names = cube.scan_names + cube.tile_names
    pixels = probe_ref.shape[1]
    planes = object_ref.shape[0]
    half = planes // 2
    across, beside = cube.tile_names[0], cube.tile_names[1]
    turn = cube.scan_names[-1]

    def probe_at(done, columns):
        bits = tuple(slice(None) if name in done else own[name] for name in names)
        return all_probe_ref.at[bits + (slice(None), columns)]

    def object_at(far, start, count):
        place = 1 - own[across] if far else own[across]
        return all_object_ref.at[place, own[beside], pl.ds(start, count)]

    halves = [pl.ds(0, pixels // 2), pl.ds(pixels // 2, pixels // 2)]
    early, late = cube.scan_names[:-1], cube.tile_names[-1:]
    orders = [early + [turn, across] + late, early + [across, turn] + late]

    cube.greet()
    own_probe = pltpu.make_async_copy(probe_ref, probe_at((), pl.ds(0, pixels)), own_sem.at[0])
    own_object = pltpu.make_async_copy(object_ref, object_at(False, 0, planes), own_sem.at[1])
    own_probe.start()
    own_object.start()

    def probe_step(step):
        copies = []
        for columns, order in zip(halves, orders):
            target = probe_at(order[:step], columns)
            source = probe_ref.at[:, columns] if step == 0 else target
            copies.append(wires.start(source, target, order[step]))
        return copies

    def settle(copies):
        for copy in copies:
            copy.wait_recv()

    moving = probe_step(0)
    first = own[turn] * half
    over = [
        wires.start(
            object_ref.at[pl.ds(first + j, 1)], object_at(False, first + j, 1), across
        )
        for j in range(half)
    ]
    near = [wires.start(object_ref, object_at(False, 0, planes), beside)]
    own_probe.wait()
    for step in range(1, len(early)):
        settle(moving)
        moving = probe_step(step)
    second = []
    for j in range(half):
        over[j].wait_recv()
        place = object_at(True, first + j, 1)
        second.append(wires.start(place, place, turn))
        near.append(wires.start(place, place, beside))
    settle(moving)
    moving = probe_step(len(early))
    other = (1 - own[turn]) * half
    for j in range(half):
        second[j].wait_recv()
        place = object_at(True, other + j, 1)
        near.append(wires.start(place, place, beside))
    for step in range(len(early) + 1, len(names)):
        settle(moving)
        moving = probe_step(step)
    settle(moving)
    settle(near)
    own_object.wait()
    wires.finish()


def gather(scan_bits, tile_bits, probe_modes, own_object):
    rows, pixels = probe_modes.shape
    planes, side, _ = own_object.shape
    bits = scan_bits + tile_bits
    copies = 2 * bits + 1 + 4 * (planes // 2)
    anywhere = pl.BlockSpec(memory_space=pl.ANY)
    return pl.pallas_call(
        functools.partial(gather_kernel, scan_bits, tile_bits),
        out_shape=(
            jax.ShapeDtypeStruct((2,) * bits + (rows, pixels), jnp.float32),
            jax.ShapeDtypeStruct((2,) * tile_bits + (planes, side, side), jnp.float32),
        ),
        in_specs=[anywhere, anywhere],
        out_specs=(anywhere, anywhere),
        scratch_shapes=[
            pltpu.SemaphoreType.DMA((copies,)),
            pltpu.SemaphoreType.DMA((copies,)),
            pltpu.SemaphoreType.DMA((2,)),
        ],
        compiler_params=pltpu.CompilerParams(
            collective_id=0, has_side_effects=True, vmem_limit_bytes=VMEM_BYTES
        ),
        name="gather",
    )(probe_modes, own_object)


def scatter_kernel(
    scan_bits, tile_bits, probe_ref, object_ref, probe_out_ref, object_out_ref,
    probe_land, object_land, send_sem, recv_sem,
):
    cube = Cube(scan_bits, tile_bits)
    wires = Wires(cube, send_sem, recv_sem)
    own = cube.own
    bits = scan_bits + tile_bits
    pixels = probe_out_ref.shape[1]
    halves, half = object_ref.shape[0], object_ref.shape[1]
    across, beside = cube.tile_names[0], cube.tile_names[1]
    turn = cube.scan_names[-1]
    rest = cube.scan_names[-2::-1]

    flows = []
    for j in range(half):
        for h in range(halves):
            middle = [across, turn] if h == 0 else [turn, across]
            order = [beside] + middle + rest
            lands = [land.at[h, j] for land in object_land]
            flows.append((order, cube.tile_names + cube.scan_names, object_ref, (h, j), (), lands, object_out_ref, (h, j)))
    for c in range(2):
        columns = pl.ds(c * (pixels // 2), pixels // 2)
        order = [beside] + (rest + [across, turn] if c == 0 else [across, turn] + rest)
        lands = [land.at[c] for land in probe_land]
        flows.append((order, cube.scan_names + cube.tile_names, probe_ref, (), (slice(None), columns), lands, probe_out_ref, (slice(None), columns)))

    def part(flow, step, kept):
        order, names, ref, front, back, lands, _, _ = flow
        names = [name for name in names if name not in order[:step]]
        place = tuple(
            (own[name] if kept else 1 - own[name]) if name == order[step] else slice(None)
            for name in names
        )
        if step == 0:
            return ref, front + place + (back if back else (slice(None), slice(None)))
        return lands[step - 1], place + (slice(None), slice(None))

    def send(flow, step):
        ref, place = part(flow, step, False)
        return wires.start(ref.at[place], flow[5][step], flow[0][step])

    cube.greet()
    moving = [send(flow, 0) for flow in flows]
    for step in range(bits):
        for number, flow in enumerate(flows):
            moving[number].wait_recv()
            ref, place = part(flow, step, True)
            land = flow[5][step]
            total = land[...] + ref[place]
            if step == bits - 1:
                flow[6][flow[7]] = total
            else:
                land[...] = total
                moving[number] = send(flow, step + 1)
    wires.finish()


def scatter(scan_bits, tile_bits, probe_total, object_total):
    rows, pixels = probe_total.shape[-2:]
    halves, half = object_total.shape[:2]
    tall, side = object_total.shape[-2:]
    bits = scan_bits + tile_bits
    copies = bits * (2 + halves * half)
    in_vmem = pl.BlockSpec(memory_space=pltpu.VMEM)
    return pl.pallas_call(
        functools.partial(scatter_kernel, scan_bits, tile_bits),
        out_shape=(
            jax.ShapeDtypeStruct((rows, pixels), jnp.float32),
            jax.ShapeDtypeStruct((halves, half, tall, side), jnp.float32),
        ),
        in_specs=[in_vmem, in_vmem],
        out_specs=(in_vmem, in_vmem),
        scratch_shapes=[
            [
                pltpu.VMEM((2,) + (2,) * (bits - 1 - step) + (rows, pixels // 2), jnp.float32)
                for step in range(bits)
            ],
            [
                pltpu.VMEM((halves, half) + (2,) * (bits - 1 - step) + (tall, side), jnp.float32)
                for step in range(bits)
            ],
            pltpu.SemaphoreType.DMA((copies,)),
            pltpu.SemaphoreType.DMA((copies,)),
        ],
        compiler_params=pltpu.CompilerParams(
            collective_id=1, has_side_effects=True, vmem_limit_bytes=VMEM_BYTES
        ),
        name="scatter",
    )(probe_total, object_total)


def body(probe_modes, object_tiles, scan_offsets, patch_tiles, amplitudes):
    tile_count = lax.axis_size("tile")
    scan_count = lax.axis_size("scan")
    rows, pixels = probe_modes.shape
    layers, side = object_tiles.shape[1], object_tiles.shape[3]
    planes = 2 * layers
    scan_bits, tile_bits = scan_count.bit_length() - 1, tile_count.bit_length() - 1
    assert scan_count == 1 << scan_bits and tile_count == 1 << tile_bits
    whole_probe, whole_object = gather(
        scan_bits, tile_bits, probe_modes, object_tiles.reshape(planes, side, side)
    )
    probe_total, object_total = misfit_gradients(
        whole_probe.reshape(2, -1, pixels, pixels),
        whole_object.reshape(tile_count, planes, side, side),
        scan_offsets,
        patch_tiles,
        amplitudes,
    )
    bits = (2,) * (scan_bits + tile_bits)
    probe_gradient, object_gradient = scatter(
        scan_bits,
        tile_bits,
        probe_total.reshape(bits + (rows, pixels)),
        object_total.reshape((2, layers) + bits + (side // scan_count, side)),
    )
    return (
        probe_gradient,
        object_gradient.reshape(1, layers, 2, side // scan_count, side),
    )


def solution(mesh):
    placed = (
        P(("scan", "tile"), None),
        P("tile", None, None, None, None),
        P(("scan", "tile"), None),
        P(("scan", "tile")),
        P(("scan", "tile"), None, None),
    )
    return jax.shard_map(
        body,
        mesh=mesh,
        in_specs=placed,
        out_specs=(P(("scan", "tile"), None), P("tile", None, None, "scan", None)),
        check_vma=False,
    )
```

```python
import functools
import math

import jax
import jax.numpy as jnp
import ml_dtypes
import numpy as np
from jax import lax
from jax.experimental import pallas as pl
from jax.experimental.pallas import tpu as pltpu
from jax.sharding import PartitionSpec as P

MESH = pl.DeviceIdType.MESH
VMEM_BYTES = 56 * 1024 * 1024


def block_tables(pixels):
    index = np.arange(pixels, dtype=np.int64)
    offset = index[:, None] - index[None, :]
    chirp = (offset * offset % (2 * pixels)) * (math.pi / pixels)
    product = (index[:, None] * index[None, :] % pixels) * (2.0 * math.pi / pixels)
    scale = 1.0 / math.sqrt(pixels)
    tables = []
    for real, imag in ((np.cos(chirp), np.sin(chirp)), (np.cos(product), -np.sin(product))):
        real, imag = real * scale, imag * scale
        whole = np.block([[real, -imag], [imag, real]]).astype(np.float32)
        whole = whole.astype(ml_dtypes.bfloat16)
        tables += [whole, np.ascontiguousarray(whole.T)]
    return np.stack(tables)


def dot(left, right):
    return jnp.dot(left, right, preferred_element_type=jnp.float32)


def misfit_kernel(
    layers, group, tile_ref, corner_ref, probe_ref, object_ref, amplitude_ref, table_ref,
    probe_grad_ref, object_grad_ref, patch_ref, piece_ref, wave_ref, bright_ref,
):
    modes, pixels = probe_ref.shape[1], probe_ref.shape[2]
    positions = amplitude_ref.shape[0]
    planes, side = object_grad_ref.shape[0], object_grad_ref.shape[3]
    wide = -(-side // 128) * 128
    tall = min(pixels + 8, side)

    def clear(plane, carry):
        for tile in range(object_grad_ref.shape[1]):
            object_grad_ref[plane, tile] = jnp.zeros((side, side), jnp.float32)
        return carry

    lax.fori_loop(0, planes, clear, 0)

    def rows_of(value):
        return jnp.concatenate([value[:pixels], value[pixels:]], axis=1)

    def columns_of(value):
        return jnp.concatenate([value[:, :pixels], value[:, pixels:]], axis=0)

    def one_position(position, carry):
        tile = tile_ref[position]
        row, column = corner_ref[position, 0], corner_ref[position, 1]
        base = pl.multiple_of(jnp.minimum(row // 8 * 8, side - tall), 8)
        shift = row - base

        def cut(plane, carry):
            rows = object_ref[tile, plane, pl.ds(base, tall), :]
            padded = jnp.concatenate([rows, jnp.zeros((tall, wide - side), jnp.float32)], axis=1)
            moved = pltpu.roll(padded, lax.rem(wide - column, wide), 1)[:, :pixels]
            patch_ref[plane] = pltpu.roll(moved, lax.rem(tall - shift, tall), 0)[:pixels]
            piece_ref[plane] = jnp.zeros((pixels, pixels), jnp.float32)
            return carry

        lax.fori_loop(0, planes, cut, 0)
        bright_ref[...] = jnp.ones((pixels, pixels), jnp.float32)

        def incoming(layer, mode):
            if layer == 0:
                return probe_ref[0, mode], probe_ref[1, mode]
            return wave_ref[layer - 1, 0, mode], wave_ref[layer - 1, 1, mode]

        def table_at(layer):
            return 0 if layer < layers - 1 else 2

        def forward(step, carry):
            chosen = [step * group + member for member in range(group)]
            for layer in range(layers):
                at = table_at(layer)
                object_real, object_imag = patch_ref[2 * layer], patch_ref[2 * layer + 1]
                halves = []
                for mode in chosen:
                    real, imag = incoming(layer, mode)
                    rounded = jnp.concatenate(
                        [
                            real * object_real - imag * object_imag,
                            real * object_imag + imag * object_real,
                        ],
                        axis=0,
                    ).astype(jnp.bfloat16)
                    halves.append(dot(table_ref[at], rounded).astype(jnp.bfloat16))
                for mode, half in zip(chosen, halves):
                    wave = dot(rows_of(half), table_ref[at + 1])
                    real, imag = wave[:, :pixels], wave[:, pixels:]
                    wave_ref[layer, 0, mode] = real
                    wave_ref[layer, 1, mode] = imag
                    if layer == layers - 1:
                        bright_ref[...] += real * real + imag * imag
            return carry

        lax.fori_loop(0, modes // group, forward, 0)
        root = jnp.sqrt(bright_ref[...])
        measured = amplitude_ref[position].astype(jnp.float32)
        bright_ref[...] = 2.0 * (root - measured) / root

        def backward(step, carry):
            chosen = [step * group + member for member in range(group)]
            factor = bright_ref[...]
            cotangents = []
            for mode in chosen:
                real = wave_ref[layers - 1, 0, mode] * factor
                imag = wave_ref[layers - 1, 1, mode] * factor
                cotangents.append(jnp.concatenate([real, imag], axis=1).astype(jnp.bfloat16))
            for layer in reversed(range(layers)):
                at = table_at(layer)
                object_real, object_imag = patch_ref[2 * layer], patch_ref[2 * layer + 1]
                halves = [dot(value, table_ref[at]).astype(jnp.bfloat16) for value in cotangents]
                cotangents = []
                for mode, half in zip(chosen, halves):
                    change = dot(table_ref[at + 1], columns_of(half))
                    change = change.astype(jnp.bfloat16).astype(jnp.float32)
                    turn_real, turn_imag = change[:pixels], change[pixels:]
                    real, imag = incoming(layer, mode)
                    piece_ref[2 * layer] += turn_real * real + turn_imag * imag
                    piece_ref[2 * layer + 1] += turn_imag * real - turn_real * imag
                    back_real = turn_real * object_real + turn_imag * object_imag
                    back_imag = turn_imag * object_real - turn_real * object_imag
                    if layer > 0:
                        cotangents.append(
                            jnp.concatenate([back_real, back_imag], axis=1).astype(jnp.bfloat16)
                        )
                    else:
                        kept = position > 0
                        probe_grad_ref[0, mode] = back_real + jnp.where(
                            kept, probe_grad_ref[0, mode], 0.0
                        )
                        probe_grad_ref[1, mode] = back_imag + jnp.where(
                            kept, probe_grad_ref[1, mode], 0.0
                        )
            return carry

        lax.fori_loop(0, modes // group, backward, 0)

        def paste(plane, carry):
            padded = jnp.concatenate(
                [piece_ref[plane], jnp.zeros((tall - pixels, pixels), jnp.float32)], axis=0
            )
            moved = jnp.concatenate(
                [pltpu.roll(padded, shift, 0), jnp.zeros((tall, wide - pixels), jnp.float32)],
                axis=1,
            )
            moved = pltpu.roll(moved, column, 1)[:, :side]
            window = (plane, tile, pl.ds(base, tall), slice(None))
            object_grad_ref[window] = object_grad_ref[window] + moved
            return carry

        lax.fori_loop(0, planes, paste, 0)
        return carry

    lax.fori_loop(0, positions, one_position, 0)


def misfit_gradients(probe_field, whole_object, scan_offsets, patch_tiles, amplitudes):
    _, modes, pixels, _ = probe_field.shape
    tiles, planes, side, _ = whole_object.shape
    layers = planes // 2
    group = next(size for size in (3, 2, 1) if modes % size == 0)
    in_vmem = pl.BlockSpec(memory_space=pltpu.VMEM)
    in_smem = pl.BlockSpec(memory_space=pltpu.SMEM)
    return pl.pallas_call(
        functools.partial(misfit_kernel, layers, group),
        out_shape=(
            jax.ShapeDtypeStruct((2, modes, pixels, pixels), jnp.float32),
            jax.ShapeDtypeStruct((planes, tiles, side, side), jnp.float32),
        ),
        in_specs=[in_smem, in_smem, in_vmem, in_vmem, in_vmem, in_vmem],
        out_specs=(in_vmem, in_vmem),
        scratch_shapes=[
            pltpu.VMEM((planes, pixels, pixels), jnp.float32),
            pltpu.VMEM((planes, pixels, pixels), jnp.float32),
            pltpu.VMEM((layers, 2, modes, pixels, pixels), jnp.float32),
            pltpu.VMEM((pixels, pixels), jnp.float32),
        ],
        compiler_params=pltpu.CompilerParams(vmem_limit_bytes=VMEM_BYTES),
        name="misfit",
    )(
        patch_tiles, scan_offsets, probe_field, whole_object, amplitudes,
        jnp.asarray(block_tables(pixels)),
    )


def two_parts(rows, pixels):
    if rows % 16 == 0:
        return [(pl.ds(c * (rows // 2), rows // 2), slice(None)) for c in range(2)]
    return [(slice(None), pl.ds(c * (pixels // 2), pixels // 2)) for c in range(2)]


def part_shape(rows, pixels):
    return (rows // 2, pixels) if rows % 16 == 0 else (rows, pixels // 2)


class Cube:
    def __init__(self, scan_bits, tile_bits):
        scan, tile = lax.axis_index("scan"), lax.axis_index("tile")
        self.scan_names = ["s%d" % bit for bit in reversed(range(scan_bits))]
        self.tile_names = ["t%d" % bit for bit in reversed(range(tile_bits))]
        self.own, self.partner = {}, {}
        for axis, letter, index, bits in (("scan", "s", scan, scan_bits), ("tile", "t", tile, tile_bits)):
            for bit in range(bits):
                value = (index // (1 << bit)) % 2
                self.own[letter + str(bit)] = value
                self.partner[letter + str(bit)] = {axis: index + (1 - 2 * value) * (1 << bit)}

    def greet(self):
        barrier = pltpu.get_barrier_semaphore()
        for target in self.partner.values():
            pl.semaphore_signal(barrier, inc=1, device_id=target, device_id_type=MESH)
        pl.semaphore_wait(barrier, len(self.partner))


class Wires:
    def __init__(self, cube, send_sem, recv_sem):
        self.cube, self.send_sem, self.recv_sem, self.used = cube, send_sem, recv_sem, 0
        self.sent = []

    def start(self, source, target, name):
        copy = pltpu.make_async_remote_copy(
            src_ref=source,
            dst_ref=target,
            send_sem=self.send_sem.at[self.used],
            recv_sem=self.recv_sem.at[self.used],
            device_id=self.cube.partner[name],
            device_id_type=MESH,
        )
        self.used += 1
        copy.start()
        self.sent.append(copy)
        return copy

    def finish(self):
        for copy in self.sent:
            copy.wait_send()


def gather_kernel(
    scan_bits, tile_bits, probe_ref, object_ref, all_probe_ref, all_object_ref,
    send_sem, recv_sem, own_sem,
):
    cube = Cube(scan_bits, tile_bits)
    wires = Wires(cube, send_sem, recv_sem)
    own = cube.own
    names = cube.scan_names + cube.tile_names
    planes = object_ref.shape[0]
    half = planes // 2
    across, beside = cube.tile_names[0], cube.tile_names[1]
    turn = cube.scan_names[-1]

    def probe_at(done, place):
        bits = tuple(slice(None) if name in done else own[name] for name in names)
        return all_probe_ref.at[bits + place]

    def object_at(far, start, count):
        place = 1 - own[across] if far else own[across]
        return all_object_ref.at[place, own[beside], pl.ds(start, count)]

    halves = two_parts(*probe_ref.shape)
    early, late = cube.scan_names[:-1], cube.tile_names[-1:]
    orders = [early + [turn, across] + late, early + [across, turn] + late]

    cube.greet()
    own_probe = pltpu.make_async_copy(probe_ref, probe_at((), (slice(None), slice(None))), own_sem.at[0])
    own_object = pltpu.make_async_copy(object_ref, object_at(False, 0, planes), own_sem.at[1])
    own_probe.start()
    own_object.start()

    def probe_step(step):
        copies = []
        for place, order in zip(halves, orders):
            target = probe_at(order[:step], place)
            source = probe_ref.at[place] if step == 0 else target
            copies.append(wires.start(source, target, order[step]))
        return copies

    def settle(copies):
        for copy in copies:
            copy.wait_recv()

    moving = probe_step(0)
    first = own[turn] * half
    over = [
        wires.start(
            object_ref.at[pl.ds(first + j, 1)], object_at(False, first + j, 1), across
        )
        for j in range(half)
    ]
    near = [wires.start(object_ref, object_at(False, 0, planes), beside)]
    own_probe.wait()
    for step in range(1, len(early)):
        settle(moving)
        moving = probe_step(step)
    second = []
    for j in range(half):
        over[j].wait_recv()
        place = object_at(True, first + j, 1)
        second.append(wires.start(place, place, turn))
        near.append(wires.start(place, place, beside))
    settle(moving)
    moving = probe_step(len(early))
    other = (1 - own[turn]) * half
    for j in range(half):
        second[j].wait_recv()
        place = object_at(True, other + j, 1)
        near.append(wires.start(place, place, beside))
    for step in range(len(early) + 1, len(names)):
        settle(moving)
        moving = probe_step(step)
    settle(moving)
    settle(near)
    own_object.wait()
    wires.finish()


def gather(scan_bits, tile_bits, probe_modes, own_object):
    rows, pixels = probe_modes.shape
    planes, side, _ = own_object.shape
    bits = scan_bits + tile_bits
    copies = 2 * bits + 1 + 4 * (planes // 2)
    anywhere = pl.BlockSpec(memory_space=pl.ANY)
    return pl.pallas_call(
        functools.partial(gather_kernel, scan_bits, tile_bits),
        out_shape=(
            jax.ShapeDtypeStruct((2,) * bits + (rows, pixels), jnp.float32),
            jax.ShapeDtypeStruct((2,) * tile_bits + (planes, side, side), jnp.float32),
        ),
        in_specs=[anywhere, anywhere],
        out_specs=(anywhere, anywhere),
        scratch_shapes=[
            pltpu.SemaphoreType.DMA((copies,)),
            pltpu.SemaphoreType.DMA((copies,)),
            pltpu.SemaphoreType.DMA((2,)),
        ],
        compiler_params=pltpu.CompilerParams(
            collective_id=0, has_side_effects=True, vmem_limit_bytes=VMEM_BYTES
        ),
        name="gather",
    )(probe_modes, own_object)


def scatter_kernel(
    scan_bits, tile_bits, probe_ref, object_ref, probe_out_ref, object_out_ref,
    probe_land, object_land, send_sem, recv_sem,
):
    cube = Cube(scan_bits, tile_bits)
    wires = Wires(cube, send_sem, recv_sem)
    own = cube.own
    bits = scan_bits + tile_bits
    halves, half = object_ref.shape[0], object_ref.shape[1]
    across, beside = cube.tile_names[0], cube.tile_names[1]
    turn = cube.scan_names[-1]
    rest = cube.scan_names[-2::-1]

    flows = []
    for j in range(half):
        for h in range(halves):
            middle = [across, turn] if h == 0 else [turn, across]
            order = [beside] + middle + rest
            lands = [land.at[h, j] for land in object_land]
            flows.append((order, cube.tile_names + cube.scan_names, object_ref, (h, j), (), lands, object_out_ref, (h, j)))
    for c, block in enumerate(two_parts(*probe_out_ref.shape)):
        order = [beside] + (rest + [across, turn] if c == 0 else [across, turn] + rest)
        lands = [land.at[c] for land in probe_land]
        flows.append((order, cube.scan_names + cube.tile_names, probe_ref, (), block, lands, probe_out_ref, block))

    def part(flow, step, kept):
        order, names, ref, front, back, lands, _, _ = flow
        names = [name for name in names if name not in order[:step]]
        place = tuple(
            (own[name] if kept else 1 - own[name]) if name == order[step] else slice(None)
            for name in names
        )
        if step == 0:
            return ref, front + place + (back if back else (slice(None), slice(None)))
        return lands[step - 1], place + (slice(None), slice(None))

    def send(flow, step):
        ref, place = part(flow, step, False)
        return wires.start(ref.at[place], flow[5][step], flow[0][step])

    cube.greet()
    moving = [send(flow, 0) for flow in flows]
    for step in range(bits):
        for number, flow in enumerate(flows):
            moving[number].wait_recv()
            ref, place = part(flow, step, True)
            land = flow[5][step]
            total = land[...] + ref[place]
            if step == bits - 1:
                flow[6][flow[7]] = total
            else:
                land[...] = total
                moving[number] = send(flow, step + 1)
    wires.finish()


def scatter(scan_bits, tile_bits, probe_total, object_total):
    rows, pixels = probe_total.shape[-2:]
    halves, half = object_total.shape[:2]
    tall, side = object_total.shape[-2:]
    bits = scan_bits + tile_bits
    copies = bits * (2 + halves * half)
    in_vmem = pl.BlockSpec(memory_space=pltpu.VMEM)
    return pl.pallas_call(
        functools.partial(scatter_kernel, scan_bits, tile_bits),
        out_shape=(
            jax.ShapeDtypeStruct((rows, pixels), jnp.float32),
            jax.ShapeDtypeStruct((halves, half, tall, side), jnp.float32),
        ),
        in_specs=[in_vmem, in_vmem],
        out_specs=(in_vmem, in_vmem),
        scratch_shapes=[
            [
                pltpu.VMEM((2,) + (2,) * (bits - 1 - step) + part_shape(rows, pixels), jnp.float32)
                for step in range(bits)
            ],
            [
                pltpu.VMEM((halves, half) + (2,) * (bits - 1 - step) + (tall, side), jnp.float32)
                for step in range(bits)
            ],
            pltpu.SemaphoreType.DMA((copies,)),
            pltpu.SemaphoreType.DMA((copies,)),
        ],
        compiler_params=pltpu.CompilerParams(
            collective_id=1, has_side_effects=True, vmem_limit_bytes=VMEM_BYTES
        ),
        name="scatter",
    )(probe_total, object_total)


def body(probe_modes, object_tiles, scan_offsets, patch_tiles, amplitudes):
    tile_count = lax.axis_size("tile")
    scan_count = lax.axis_size("scan")
    rows, pixels = probe_modes.shape
    layers, side = object_tiles.shape[1], object_tiles.shape[3]
    planes = 2 * layers
    scan_bits, tile_bits = scan_count.bit_length() - 1, tile_count.bit_length() - 1
    assert scan_count == 1 << scan_bits and tile_count == 1 << tile_bits
    whole_probe, whole_object = gather(
        scan_bits, tile_bits, probe_modes, object_tiles.reshape(planes, side, side)
    )
    probe_total, object_total = misfit_gradients(
        whole_probe.reshape(2, -1, pixels, pixels),
        whole_object.reshape(tile_count, planes, side, side),
        scan_offsets,
        patch_tiles,
        amplitudes,
    )
    bits = (2,) * (scan_bits + tile_bits)
    probe_gradient, object_gradient = scatter(
        scan_bits,
        tile_bits,
        probe_total.reshape(bits + (rows, pixels)),
        object_total.reshape((2, layers) + bits + (side // scan_count, side)),
    )
    return (
        probe_gradient,
        object_gradient.reshape(1, layers, 2, side // scan_count, side),
    )


def solution(mesh):
    placed = (
        P(("scan", "tile"), None),
        P("tile", None, None, None, None),
        P(("scan", "tile"), None),
        P(("scan", "tile")),
        P(("scan", "tile"), None, None),
    )
    return jax.shard_map(
        body,
        mesh=mesh,
        in_specs=placed,
        out_specs=(P(("scan", "tile"), None), P("tile", None, None, "scan", None)),
        check_vma=False,
    )
```
